256 devices in a mesh: island: 16 (over z_hi, x, core), zero: 16 (over y, z_lo).
Axes of the slice: x: 4, y: 4, z: 8 (z_hi: 2, z_lo: 4; z = z_hi * 4 + z_lo), core: 2. Of those that a mesh axis runs over, the one named last changes fastest.
Arguments:
- tokens: bfloat16 [131072, 8192], P(('island', 'zero')), may hold values from -6 to 6
- norm_gain: float32 [8192], replicated, may hold values from 0.1 to 1.9
- outer_params: float32 [8192, 512], P('zero'), may hold values from -6 to 6
- momentum: float32 [8192, 512], P('zero'), may hold values from -3 to 3
- local_weights: float32 [16, 8192, 512], P('island', 'zero'), may hold values from -6 to 6
Outputs:
- keys: bfloat16 [131072, 512], P(('island', 'zero'))
- params_out: float32 [8192, 512], P('zero')
- momentum_out: float32 [8192, 512], P('zero')
- mixed: float32 [16, 8192, 512], P('island', 'zero')
The draws below stay inside these ranges and needn't reach their ends.
All inputs are finite; a program needn't handle non-finite values.
Results may differ from the reference program's by a relative error of at most 0.0057.
Values may be sent and summed in bfloat16 or wider, within the bound.
No kernel may reach another device: no remote copies, remote signals or barrier semaphores. Data moves between devices by JAX's collectives and lax.ppermute only.
A program may use at most 64 MiB of HBM per device.

```python
import math
import jax
import jax.numpy as jnp
from jax import lax

D = 8192
TOK_DEV = 512
K = 512
ISLANDS = 16
TOKENS = 131072


def shard_levels(stream_key, extent, cuts, low, largest):
    factor_of, own = 1.0, jax.random.fold_in(stream_key, 6)
    for position, parts in cuts:
        heights = jnp.exp(jax.random.uniform(jax.random.fold_in(own, position), (parts,), jnp.float32, low / len(cuts), largest / len(cuts)))
        factor_of = factor_of * jnp.repeat(heights, extent[position] // parts).reshape([-1 if axis == position else 1 for axis in range(len(extent))])
    return factor_of


def centred(stream_key, extent, deviation, bound, cuts=(), held_as=jnp.bfloat16):
    values = jax.random.normal(stream_key, extent, jnp.float32) * deviation
    if len(cuts) > 0:
        values = shard_levels(stream_key, extent, cuts, -0.22, 0.18) * values
    return jnp.clip(values, min=-bound, max=bound).astype(held_as)


def setup_inputs(seed: int = 0) -> dict:
    arg_keys = jax.random.split(jax.random.key(seed), 6)
    tokens = centred(arg_keys[0], (TOKENS, D), 1.0, 6.0, ((0, 256),))
    norm_gain = jnp.clip(1.0 + 0.18 * jax.random.normal(arg_keys[1], (D,), jnp.float32), 0.1, 1.9)
    outer_params = centred(arg_keys[2], (D, K), 1.0, 6.0, ((0, 16),), jnp.float32)
    momentum = centred(arg_keys[3], (D, K), 0.5, 3.0, ((0, 16),), jnp.float32)
    local_weights = centred(arg_keys[4], (ISLANDS, D, K), 1.0, 6.0, ((0, 16), (1, 16)), jnp.float32)
    return dict(tokens=tokens, norm_gain=norm_gain, outer_params=outer_params, momentum=momentum, local_weights=local_weights)


epsilon = 1e-05
outer_momentum = 0.9
outer_rate = 0.7
mix_share = 0.5

def key_block(block, norm_gain, weight_bf):
    values = block.astype(jnp.float32)
    scale = lax.rsqrt(lax.optimization_barrier(jnp.mean(values * values, axis=-1, keepdims=True)) + epsilon)
    normed = (values * scale * norm_gain).astype(jnp.bfloat16)
    summed = jnp.dot(normed, weight_bf, preferred_element_type=jnp.float32)
    return (summed * (1.0 / math.sqrt(D))).astype(jnp.bfloat16)

def island_keys(pair, norm_gain):
    island_tokens, copy = pair
    weight_bf = copy.astype(jnp.bfloat16)
    blocks = island_tokens.reshape(-1, TOK_DEV, D)
    return lax.map(lambda block: key_block(block, norm_gain, weight_bf), blocks).reshape(-1, K)

def reference(tokens, norm_gain, outer_params, momentum, local_weights):
    grouped = tokens.reshape(ISLANDS, -1, D)
    keys = lax.map(lambda pair: island_keys(pair, norm_gain), (grouped, local_weights)).reshape(-1, K)
    average = lax.optimization_barrier(jnp.sum(local_weights.astype(jnp.float32), axis=0)) / ISLANDS
    delta = outer_params - average
    momentum_out = outer_momentum * momentum + delta
    params_out = outer_params - outer_rate * (delta + outer_momentum * momentum_out)
    mixed = mix_share * local_weights.astype(jnp.float32) + (1.0 - mix_share) * params_out[None]
    return (keys, params_out, momentum_out, mixed)
```

```python
import math

import jax
import jax.numpy as jnp
from jax import lax
from jax.experimental import pallas as pl
from jax.experimental.pallas import tpu as pltpu
from jax.sharding import PartitionSpec as P

D = 8192
ROWS = 512

epsilon = 1e-05
outer_momentum = 0.9
outer_rate = 0.7
mix_share = 0.5


def ring_pairs(first):
    pairs = []
    for island in range(16):
        for zero in range(16):
            y, z = divmod(zero, 4)
            partner = y ^ 1 if (island % 2 == 0) == first else 3 - y
            pairs.append((island * 16 + zero, island * 16 + partner * 4 + z))
    return pairs


def swap(bits):
    return [(i, i ^ bits) for i in range(16)]


BOTH = ("island", "zero")


class Order:
    def __init__(self):
        self.last = None

    def __call__(self, value):
        if self.last is not None:
            value = lax.optimization_barrier((value, self.last))[0]
        self.last = value
        return value


def outer_update(params_part, momentum_part, delta):
    momentum_new = outer_momentum * momentum_part + delta
    params_new = params_part - outer_rate * (delta + outer_momentum * momentum_new)
    return (params_new, momentum_new)


CHUNK = 64


def scale_kernel(tokens_ref, scale_ref, held, arrived):
    chunks = tokens_ref.shape[0] // CHUNK

    def fetch(i):
        rows = pl.ds(pl.multiple_of(i * CHUNK, CHUNK), CHUNK)
        return pltpu.make_async_copy(
            tokens_ref.at[rows, :], held.at[lax.rem(i, 2)], arrived.at[lax.rem(i, 2)]
        )

    fetch(0).start()

    @pl.loop(0, chunks)
    def _(i):
        @pl.when(i + 1 < chunks)
        def _():
            fetch(i + 1).start()

        fetch(i).wait()
        values = held[lax.rem(i, 2)].astype(jnp.float32)
        mean = jnp.sum(values * values, axis=-1, keepdims=True) * (1.0 / D)
        rows = pl.ds(pl.multiple_of(i * CHUNK, CHUNK), CHUNK)
        scale_ref[rows, :] = lax.rsqrt(mean + epsilon)


def token_scale(tokens):
    count, width = tokens.shape
    return pl.pallas_call(
        scale_kernel,
        out_shape=jax.ShapeDtypeStruct((count, 1), jnp.float32),
        in_specs=[pl.BlockSpec(memory_space=pltpu.HBM)],
        out_specs=pl.BlockSpec(memory_space=pltpu.VMEM),
        scratch_shapes=[
            pltpu.VMEM((2, CHUNK, width), tokens.dtype),
            pltpu.SemaphoreType.DMA((2,)),
        ],
        compiler_params=pltpu.CompilerParams(vmem_limit_bytes=8 * 1024 * 1024),
        cost_estimate=pl.CostEstimate(
            flops=3 * count * width, bytes_accessed=2 * count * width, transcendentals=0
        ),
        name="token_scale",
    )(tokens)


def send(name, value, axis, pairs):
    with jax.named_scope(name):
        return lax.ppermute(value, axis, pairs)


def split(value, high):
    half = value.shape[0] // 2
    low_part, high_part = value[:half], value[half:]
    return jnp.where(high, high_part, low_part), jnp.where(high, low_part, high_part)


def join(mine, other, high):
    return jnp.concatenate([jnp.where(high, other, mine), jnp.where(high, mine, other)])


def body(tokens, norm_gain, outer_params, momentum, local_weights):
    own_copy = local_weights[0]
    me = lax.axis_index("zero")
    y, z = me // 4, me % 4
    island = lax.axis_index("island")
    core, x = island % 2, island // 2 % 4
    near_y = jnp.where(core == 0, y ^ 1, 3 - y)
    far_y = jnp.where(core == 0, 3 - y, y ^ 1)
    order = Order()
    summed = [0.0]

    def add_product(name, block, row, column):
        start = (row * 4 + column) * ROWS
        with jax.named_scope(name):
            part = lax.dynamic_slice(tokens, (0, start), (tokens.shape[0], ROWS))
            gain = lax.dynamic_slice(norm_gain, (start,), (ROWS,))
            part = (part.astype(jnp.float32) * scale * gain).astype(jnp.bfloat16)
            summed[0] = order(
                summed[0] + jnp.dot(part, block, preferred_element_type=jnp.float32)
            )

    def add_pair(name, pair, column):
        add_product(name, pair[:ROWS], far_y, column)
        add_product(name, pair[ROWS:], y ^ 2, column)

    def pair(block, near):
        return order(jnp.concatenate([block, near]))

    first, second = ring_pairs(True), ring_pairs(False)
    own = order(own_copy.astype(jnp.bfloat16))
    a0 = send("A0", own, BOTH, first)
    z2 = send("Z2", own, "zero", swap(2))
    z1 = send("Z1", own, "zero", swap(1))
    keep, give = split(order(outer_params - own_copy), core == 1)
    k1 = send("K1", order(give), "island", swap(1))

    a0 = order(a0)
    f0 = send("F0", pair(own, a0), BOTH, second)
    total = order(keep + order(k1))
    keep, give = split(total, x % 2 == 1)
    k2 = send("K2", order(give), "island", swap(2))

    scale = order(token_scale(order(tokens)))

    total = order(keep + order(k2))
    keep, give = split(total, x // 2 == 1)
    k3 = send("K3", order(give), "island", swap(4))

    z1 = order(z1)
    a1 = send("A1", z1, BOTH, first)
    z2 = order(z2)
    a2 = send("A2", z2, BOTH, first)
    total = order(keep + order(k3))
    high = send("HIGH", total, "island", swap(8))
    z3 = send("Z3", order(own), "zero", swap(3))
    f0 = order(f0)
    zf = send("ZF", f0, "zero", swap(1))

    add_product("dot0", own, y, z)
    add_product("dot0", a0, near_y, z)
    add_pair("dot0", f0, z)
    add_product("dot1", z1, y, z ^ 1)
    add_product("dot2", z2, y, z ^ 2)

    a1 = order(a1)
    a2 = order(a2)
    f2 = send("F2", pair(z2, a2), BOTH, second)
    add_product("dot1", a1, near_y, z ^ 1)
    add_product("dot2", a2, near_y, z ^ 2)

    total = order(total + order(high))
    k4 = send("K4", total, "island", swap(4))

    z3 = order(z3)
    a3 = send("A3", z3, BOTH, first)
    add_product("dot3", z3, y, z ^ 3)
    total = order(join(total, order(k4), x // 2 == 1))
    k5 = send("K5", total, "island", swap(2))

    f2 = order(f2)
    add_pair("dot2", f2, z ^ 2)

    a3 = order(a3)
    f3 = send("F3", pair(z3, a3), BOTH, second)
    add_product("dot3", a3, near_y, z ^ 3)

    total = order(join(total, order(k5), x % 2 == 1))
    k6 = send("K6", total, "island", swap(1))

    add_pair("dot1", order(zf), z ^ 1)

    total = order(join(total, order(k6), core == 1))
    islands = lax.axis_size("island")
    params_out, momentum_out = outer_update(outer_params, momentum, total / islands)
    mixed = mix_share * local_weights + (1.0 - mix_share) * params_out[None]
    params_out, momentum_out, mixed = lax.optimization_barrier(
        (params_out, momentum_out, mixed)
    )
    order.last = (order.last, params_out)

    add_pair("dot3", order(f3), z ^ 3)
    keys = (summed[0] * (1.0 / math.sqrt(D))).astype(jnp.bfloat16)
    return (keys, params_out, momentum_out, mixed)


def solution(mesh):
    placed = (
        P(("island", "zero"), None),
        P(),
        P("zero", None),
        P("zero", None),
        P("island", "zero", None),
    )
    return jax.shard_map(
        body,
        mesh=mesh,
        in_specs=placed,
        out_specs=(
            P(("island", "zero"), None),
            P("zero", None),
            P("zero", None),
            P("island", "zero", None),
        ),
        check_vma=False,
    )
```

```python
import math

import jax
import jax.numpy as jnp
from jax import lax
from jax.experimental import pallas as pl
from jax.experimental.pallas import tpu as pltpu
from jax.sharding import PartitionSpec as P

D = 8192
ROWS = 512

epsilon = 1e-05
outer_momentum = 0.9
outer_rate = 0.7
mix_share = 0.5


def ring_pairs(first):
    pairs = []
    for island in range(16):
        for zero in range(16):
            y, z = divmod(zero, 4)
            partner = y ^ 1 if (island % 2 == 0) == first else 3 - y
            pairs.append((island * 16 + zero, island * 16 + partner * 4 + z))
    return pairs


def swap(bits):
    return [(i, i ^ bits) for i in range(16)]


def middle_swap():
    pairs = []
    for island in range(16):
        for zero in range(16):
            y, z = divmod(zero, 4)
            there = island if z in (1, 2) else island ^ 8
            pairs.append((island * 16 + zero, there * 16 + y * 4 + 3 - z))
    return pairs


BOTH = ("island", "zero")


class Order:
    def __init__(self):
        self.last = None

    def __call__(self, value):
        if self.last is not None:
            value = lax.optimization_barrier((value, self.last))[0]
        self.last = value
        return value


def outer_update(params_part, momentum_part, delta):
    momentum_new = outer_momentum * momentum_part + delta
    params_new = params_part - outer_rate * (delta + outer_momentum * momentum_new)
    return (params_new, momentum_new)


CHUNK = 64
DEPTH = 4


def norm_kernel(tokens_ref, gain_ref, normed_ref, held, arrived):
    step, steps = pl.program_id(0), pl.num_programs(0)

    def fetch(i):
        rows = pl.ds(pl.multiple_of(i * CHUNK, CHUNK), CHUNK)
        slot = lax.rem(i, DEPTH)
        return pltpu.make_async_copy(tokens_ref.at[rows, :], held.at[slot], arrived.at[slot])

    @pl.when(step == 0)
    def _():
        for i in range(DEPTH - 1):
            fetch(i).start()

    @pl.when(step + DEPTH - 1 < steps)
    def _():
        fetch(step + DEPTH - 1).start()

    fetch(step).wait()
    values = held[lax.rem(step, DEPTH)].astype(jnp.float32)
    mean = jnp.sum(values * values, axis=-1, keepdims=True) * (1.0 / D)
    scale = lax.rsqrt(mean + epsilon)
    normed_ref[...] = (values * scale * gain_ref[...]).astype(jnp.bfloat16)


def normalise(tokens, gain):
    count, width = tokens.shape
    return pl.pallas_call(
        norm_kernel,
        out_shape=jax.ShapeDtypeStruct(tokens.shape, tokens.dtype),
        grid=(count // CHUNK,),
        in_specs=[
            pl.BlockSpec(memory_space=pltpu.HBM),
            pl.BlockSpec((1, width), lambda i: (0, 0)),
        ],
        out_specs=pl.BlockSpec((CHUNK, width), lambda i: (i, 0)),
        scratch_shapes=[
            pltpu.VMEM((DEPTH, CHUNK, width), tokens.dtype),
            pltpu.SemaphoreType.DMA((DEPTH,)),
        ],
        compiler_params=pltpu.CompilerParams(vmem_limit_bytes=12 * 1024 * 1024),
        cost_estimate=pl.CostEstimate(
            flops=6 * count * width, bytes_accessed=4 * count * width, transcendentals=0
        ),
        name="normalise",
    )(pltpu.with_memory_space_constraint(tokens, pltpu.HBM), gain)


def send(name, value, axis, pairs):
    with jax.named_scope(name):
        return lax.ppermute(value, axis, pairs)


def split(value, high):
    half = value.shape[0] // 2
    low_part, high_part = value[:half], value[half:]
    return jnp.where(high, high_part, low_part), jnp.where(high, low_part, high_part)


def join(mine, other, high):
    return jnp.concatenate([jnp.where(high, other, mine), jnp.where(high, mine, other)])


def body(tokens, norm_gain, outer_params, momentum, local_weights):
    own_copy = local_weights[0]
    me = lax.axis_index("zero")
    y, z = me // 4, me % 4
    island = lax.axis_index("island")
    core, x = island % 2, island // 2 % 4
    near_y = jnp.where(core == 0, y ^ 1, 3 - y)
    far_y = jnp.where(core == 0, 3 - y, y ^ 1)
    order = Order()
    summed = [0.0]

    def add_product(name, block, row, column):
        start = (row * 4 + column) * ROWS
        with jax.named_scope(name):
            part = lax.dynamic_slice(normed, (0, start), (normed.shape[0], ROWS))
            summed[0] = order(
                summed[0] + jnp.dot(part, block, preferred_element_type=jnp.float32)
            )

    first, second = ring_pairs(True), ring_pairs(False)
    inner = (z == 1) | (z == 2)

    own = order(own_copy.astype(jnp.bfloat16))
    z1 = send("Z1", own, "zero", swap(1))
    m1 = send("M1", own, BOTH, middle_swap())
    a0 = send("A0", own, BOTH, first)
    b0 = send("B0", own, BOTH, second)
    keep, give = split(order(outer_params - own_copy), core == 1)
    k1 = send("K1", order(give), "island", swap(1))
    a0 = order(a0)
    c0 = send("C0", a0, BOTH, second)
    b0 = order(b0)
    m1 = order(m1)
    e2 = send("E2", m1, "zero", swap(1))
    z1 = order(z1)
    m2 = send("M2", z1, BOTH, middle_swap())
    a1 = send("A1", z1, BOTH, first)
    total = order(keep + order(k1))
    keep, give = split(total, x % 2 == 1)
    k2 = send("K2", order(give), "island", swap(2))
    normed = order(normalise(tokens, order(norm_gain[None])))
    total = order(keep + order(k2))
    b1 = send("B1", order(z1), BOTH, second)
    keep, give = split(total, x // 2 == 1)
    k3 = send("K3", order(give), "island", swap(4))
    c0 = order(c0)
    m2 = order(m2)
    s2 = order(jnp.where(inner, m2, order(e2)))
    a2 = send("A2", s2, BOTH, first)
    b2 = send("B2", s2, BOTH, second)
    e3 = send("E3", m2, "zero", swap(1))
    a1 = order(a1)
    total = order(keep + order(k3))
    high = send("HIGH", order(total), "island", swap(8))
    add_product("dot0", own, y, z)
    add_product("dot0", a0, near_y, z)
    a2 = order(a2)
    c2 = send("C2", a2, BOTH, second)
    s3 = order(jnp.where(inner, m1, order(e3)))
    a3 = send("A3", s3, BOTH, first)
    b3 = send("B3", s3, BOTH, second)
    b1 = order(b1)
    c1 = send("ZC", order(c0), "zero", swap(1))
    add_product("dot0", b0, far_y, z)
    add_product("dot0", c0, y ^ 2, z)
    add_product("dot1", z1, y, z ^ 1)
    add_product("dot1", a1, near_y, z ^ 1)
    add_product("dot1", b1, far_y, z ^ 1)
    add_product("dot2", s2, y, z ^ 2)
    total = order(total + order(high))
    k4 = send("K4", total, "island", swap(4))
    b2 = order(b2)
    add_product("dot2", a2, near_y, z ^ 2)
    add_product("dot2", b2, far_y, z ^ 2)
    add_product("dot3", s3, y, z ^ 3)
    c2 = order(c2)
    total = order(join(total, order(k4), x // 2 == 1))
    k5 = send("K5", total, "island", swap(2))
    a3 = order(a3)
    c3 = send("C3", a3, BOTH, second)
    add_product("dot2", c2, y ^ 2, z ^ 2)
    add_product("dot3", a3, near_y, z ^ 3)
    add_product("dot3", order(b3), far_y, z ^ 3)
    total = order(join(total, order(k5), x % 2 == 1))
    k6 = send("K6", total, "island", swap(1))
    add_product("dot1", order(c1), y ^ 2, z ^ 1)
    add_product("dot3", order(c3), y ^ 2, z ^ 3)
    keys = order((summed[0] * (1.0 / math.sqrt(D))).astype(jnp.bfloat16))
    total = order(join(total, order(k6), core == 1))
    islands = lax.axis_size("island")
    params_out, momentum_out = outer_update(outer_params, momentum, total / islands)
    mixed = mix_share * local_weights + (1.0 - mix_share) * params_out[None]
    return (keys, params_out, momentum_out, mixed)


def solution(mesh):
    placed = (
        P(("island", "zero"), None),
        P(),
        P("zero", None),
        P("zero", None),
        P("island", "zero", None),
    )
    return jax.shard_map(
        body,
        mesh=mesh,
        in_specs=placed,
        out_specs=(
            P(("island", "zero"), None),
            P("zero", None),
            P("zero", None),
            P("island", "zero", None),
        ),
        check_vma=False,
    )
```

```python
import math

import jax
import jax.numpy as jnp
from jax import lax
from jax.experimental import pallas as pl
from jax.experimental.pallas import tpu as pltpu
from jax.sharding import PartitionSpec as P

D = 8192
ROWS = 512

epsilon = 1e-05
outer_momentum = 0.9
outer_rate = 0.7
mix_share = 0.5


def ring_pairs(first):
    pairs = []
    for island in range(16):
        for zero in range(16):
            y, z = divmod(zero, 4)
            partner = y ^ 1 if (island % 2 == 0) == first else 3 - y
            pairs.append((island * 16 + zero, island * 16 + partner * 4 + z))
    return pairs


def swap(bits):
    return [(i, i ^ bits) for i in range(16)]


def middle_swap():
    pairs = []
    for island in range(16):
        for zero in range(16):
            y, z = divmod(zero, 4)
            inner = z in (1, 2)
            target = (island, y * 4 + 3 - z) if inner else (island ^ 1, zero)
            pairs.append((island * 16 + zero, target[0] * 16 + target[1]))
    return pairs


BOTH = ("island", "zero")


class Order:
    def __init__(self):
        self.last = None

    def __call__(self, value):
        if self.last is not None:
            value = lax.optimization_barrier((value, self.last))[0]
        self.last = value
        return value


def outer_update(params_part, momentum_part, delta):
    momentum_new = outer_momentum * momentum_part + delta
    params_new = params_part - outer_rate * (delta + outer_momentum * momentum_new)
    return (params_new, momentum_new)


CHUNK = 64
DEPTH = 4


def norm_kernel(tokens_ref, gain_ref, normed_ref, held, arrived):
    step, steps = pl.program_id(0), pl.num_programs(0)

    def fetch(i):
        rows = pl.ds(pl.multiple_of(i * CHUNK, CHUNK), CHUNK)
        slot = lax.rem(i, DEPTH)
        return pltpu.make_async_copy(tokens_ref.at[rows, :], held.at[slot], arrived.at[slot])

    @pl.when(step == 0)
    def _():
        for i in range(DEPTH - 1):
            fetch(i).start()

    @pl.when(step + DEPTH - 1 < steps)
    def _():
        fetch(step + DEPTH - 1).start()

    fetch(step).wait()
    values = held[lax.rem(step, DEPTH)].astype(jnp.float32)
    mean = jnp.sum(values * values, axis=-1, keepdims=True) * (1.0 / D)
    scale = lax.rsqrt(mean + epsilon)
    normed_ref[...] = (values * scale * gain_ref[...]).astype(jnp.bfloat16)


def normalise(tokens, gain):
    count, width = tokens.shape
    return pl.pallas_call(
        norm_kernel,
        out_shape=jax.ShapeDtypeStruct(tokens.shape, tokens.dtype),
        grid=(count // CHUNK,),
        in_specs=[
            pl.BlockSpec(memory_space=pltpu.HBM),
            pl.BlockSpec((1, width), lambda i: (0, 0)),
        ],
        out_specs=pl.BlockSpec((CHUNK, width), lambda i: (i, 0)),
        scratch_shapes=[
            pltpu.VMEM((DEPTH, CHUNK, width), tokens.dtype),
            pltpu.SemaphoreType.DMA((DEPTH,)),
        ],
        compiler_params=pltpu.CompilerParams(vmem_limit_bytes=12 * 1024 * 1024),
        cost_estimate=pl.CostEstimate(
            flops=6 * count * width, bytes_accessed=4 * count * width, transcendentals=0
        ),
        name="normalise",
    )(pltpu.with_memory_space_constraint(tokens, pltpu.HBM), gain)


def send(name, value, axis, pairs):
    with jax.named_scope(name):
        return lax.ppermute(value, axis, pairs)


def split(value, high):
    half = value.shape[0] // 2
    low_part, high_part = value[:half], value[half:]
    return jnp.where(high, high_part, low_part), jnp.where(high, low_part, high_part)


def join(mine, other, high):
    return jnp.concatenate([jnp.where(high, other, mine), jnp.where(high, mine, other)])


def body(tokens, norm_gain, outer_params, momentum, local_weights):
    own_copy = local_weights[0]
    me = lax.axis_index("zero")
    y, z = me // 4, me % 4
    island = lax.axis_index("island")
    core, x = island % 2, island // 2 % 4
    near_y = jnp.where(core == 0, y ^ 1, 3 - y)
    far_y = jnp.where(core == 0, 3 - y, y ^ 1)
    order = Order()
    summed = [0.0]

    def add_product(name, block, row, column):
        start = (row * 4 + column) * ROWS
        with jax.named_scope(name):
            part = lax.dynamic_slice(normed, (0, start), (normed.shape[0], ROWS))
            summed[0] = order(
                summed[0] + jnp.dot(part, block, preferred_element_type=jnp.float32)
            )

    first, second = ring_pairs(True), ring_pairs(False)
    inner = (z == 1) | (z == 2)

    own = order(own_copy.astype(jnp.bfloat16))
    z1 = send("Z1", own, "zero", swap(1))
    m1 = send("M1", own, BOTH, middle_swap())
    a0 = send("A0", own, BOTH, first)
    b0 = send("B0", own, BOTH, second)
    keep, give = split(order(outer_params - own_copy), core == 1)
    k1 = send("K1", order(give), "island", swap(1))
    a0 = order(a0)
    c0 = send("C0", a0, BOTH, second)
    b0 = order(b0)
    m1 = order(m1)
    e2 = send("E2", m1, "zero", swap(1))
    z1 = order(z1)
    m2 = send("M2", z1, BOTH, middle_swap())
    a1 = send("A1", z1, BOTH, first)
    total = order(keep + order(k1))
    keep, give = split(total, x % 2 == 1)
    k2 = send("K2", order(give), "island", swap(2))
    normed = order(normalise(tokens, order(norm_gain[None])))
    total = order(keep + order(k2))
    c0 = order(c0)
    m2 = order(m2)
    s2 = order(jnp.where(inner, m2, order(e2)))
    a2 = send("A2", s2, BOTH, first)
    b2 = send("B2", s2, BOTH, second)
    e3 = send("E3", m2, "zero", swap(1))
    a1 = order(a1)
    keep, give = split(total, x // 2 == 1)
    k3 = send("K3", order(give), "island", swap(4))
    add_product("dot0", own, y, z)
    add_product("dot0", a0, near_y, z)
    total = order(keep + order(k3))
    high = send("HIGH", order(total), "island", swap(8))
    rest = order(jnp.concatenate([b0, c0]))
    a2 = order(a2)
    c2 = send("C2", a2, BOTH, second)
    s3 = order(jnp.where(inner, m1, order(e3)))
    a3 = send("A3", s3, BOTH, first)
    b3 = send("B3", s3, BOTH, second)
    rest = send("ZBC", order(rest), "zero", swap(1))
    add_product("dot0", b0, far_y, z)
    add_product("dot0", c0, y ^ 2, z)
    add_product("dot1", z1, y, z ^ 1)
    add_product("dot1", a1, near_y, z ^ 1)
    add_product("dot2", s2, y, z ^ 2)
    total = order(total + order(high))
    k4 = send("K4", total, "island", swap(4))
    b2 = order(b2)
    add_product("dot2", a2, near_y, z ^ 2)
    add_product("dot2", b2, far_y, z ^ 2)
    add_product("dot3", s3, y, z ^ 3)
    total = order(join(total, order(k4), x // 2 == 1))
    k5 = send("K5", total, "island", swap(2))
    a3 = order(a3)
    c3 = send("C3", a3, BOTH, second)
    add_product("dot3", a3, near_y, z ^ 3)
    add_product("dot2", order(c2), y ^ 2, z ^ 2)
    add_product("dot3", order(b3), far_y, z ^ 3)
    total = order(join(total, order(k5), x % 2 == 1))
    k6 = send("K6", total, "island", swap(1))
    rest = order(rest)
    add_product("dot1", rest[:ROWS], far_y, z ^ 1)
    add_product("dot1", rest[ROWS:], y ^ 2, z ^ 1)
    add_product("dot3", order(c3), y ^ 2, z ^ 3)
    keys = order((summed[0] * (1.0 / math.sqrt(D))).astype(jnp.bfloat16))
    total = order(join(total, order(k6), core == 1))
    islands = lax.axis_size("island")
    params_out, momentum_out = outer_update(outer_params, momentum, total / islands)
    mixed = mix_share * local_weights + (1.0 - mix_share) * params_out[None]
    return (keys, params_out, momentum_out, mixed)


def solution(mesh):
    placed = (
        P(("island", "zero"), None),
        P(),
        P("zero", None),
        P("zero", None),
        P("island", "zero", None),
    )
    return jax.shard_map(
        body,
        mesh=mesh,
        in_specs=placed,
        out_specs=(
            P(("island", "zero"), None),
            P("zero", None),
            P("zero", None),
            P("island", "zero", None),
        ),
        check_vma=False,
    )
```

```python
import math

import jax
import jax.numpy as jnp
from jax import lax
from jax.experimental import pallas as pl
from jax.experimental.pallas import tpu as pltpu
from jax.sharding import PartitionSpec as P

D = 8192
ROWS = 512

epsilon = 1e-05
outer_momentum = 0.9
outer_rate = 0.7
mix_share = 0.5


def ring_pairs(first):
    pairs = []
    for island in range(16):
        for zero in range(16):
            y, z = divmod(zero, 4)
            partner = y ^ 1 if (island % 2 == 0) == first else 3 - y
            pairs.append((island * 16 + zero, island * 16 + partner * 4 + z))
    return pairs


def swap(bits):
    return [(i, i ^ bits) for i in range(16)]


def middle_swap():
    pairs = []
    for island in range(16):
        for zero in range(16):
            y, z = divmod(zero, 4)
            inner = z in (1, 2)
            target = (island, y * 4 + 3 - z) if inner else (island ^ 1, zero)
            pairs.append((island * 16 + zero, target[0] * 16 + target[1]))
    return pairs


BOTH = ("island", "zero")


class Order:
    def __init__(self):
        self.last = None

    def __call__(self, value):
        if self.last is not None:
            value = lax.optimization_barrier((value, self.last))[0]
        self.last = value
        return value


def outer_update(params_part, momentum_part, delta):
    momentum_new = outer_momentum * momentum_part + delta
    params_new = params_part - outer_rate * (delta + outer_momentum * momentum_new)
    return (params_new, momentum_new)


CHUNK = 64
DEPTH = 4


def norm_kernel(tokens_ref, gain_ref, normed_ref, held, arrived):
    step, steps = pl.program_id(0), pl.num_programs(0)

    def fetch(i):
        rows = pl.ds(pl.multiple_of(i * CHUNK, CHUNK), CHUNK)
        slot = lax.rem(i, DEPTH)
        return pltpu.make_async_copy(tokens_ref.at[rows, :], held.at[slot], arrived.at[slot])

    @pl.when(step == 0)
    def _():
        for i in range(DEPTH - 1):
            fetch(i).start()

    @pl.when(step + DEPTH - 1 < steps)
    def _():
        fetch(step + DEPTH - 1).start()

    fetch(step).wait()
    values = held[lax.rem(step, DEPTH)].astype(jnp.float32)
    mean = jnp.sum(values * values, axis=-1, keepdims=True) * (1.0 / D)
    scale = lax.rsqrt(mean + epsilon)
    normed_ref[...] = (values * scale * gain_ref[...]).astype(jnp.bfloat16)


def normalise(tokens, gain):
    count, width = tokens.shape
    return pl.pallas_call(
        norm_kernel,
        out_shape=jax.ShapeDtypeStruct(tokens.shape, tokens.dtype),
        grid=(count // CHUNK,),
        in_specs=[
            pl.BlockSpec(memory_space=pltpu.HBM),
            pl.BlockSpec((1, width), lambda i: (0, 0)),
        ],
        out_specs=pl.BlockSpec((CHUNK, width), lambda i: (i, 0)),
        scratch_shapes=[
            pltpu.VMEM((DEPTH, CHUNK, width), tokens.dtype),
            pltpu.SemaphoreType.DMA((DEPTH,)),
        ],
        compiler_params=pltpu.CompilerParams(vmem_limit_bytes=12 * 1024 * 1024),
        cost_estimate=pl.CostEstimate(
            flops=6 * count * width, bytes_accessed=4 * count * width, transcendentals=0
        ),
        name="normalise",
    )(pltpu.with_memory_space_constraint(tokens, pltpu.HBM), gain)


def send(name, value, axis, pairs):
    with jax.named_scope(name):
        return lax.ppermute(value, axis, pairs)


def split(value, high):
    half = value.shape[0] // 2
    low_part, high_part = value[:half], value[half:]
    return jnp.where(high, high_part, low_part), jnp.where(high, low_part, high_part)


def join(mine, other, high):
    return jnp.concatenate([jnp.where(high, other, mine), jnp.where(high, mine, other)])


def body(tokens, norm_gain, outer_params, momentum, local_weights):
    own_copy = local_weights[0]
    me = lax.axis_index("zero")
    y, z = me // 4, me % 4
    island = lax.axis_index("island")
    core, x = island % 2, island // 2 % 4
    near_y = jnp.where(core == 0, y ^ 1, 3 - y)
    far_y = jnp.where(core == 0, 3 - y, y ^ 1)
    order = Order()
    summed = [0.0]

    def add_product(name, block, row, column):
        start = (row * 4 + column) * ROWS
        with jax.named_scope(name):
            part = lax.dynamic_slice(normed, (0, start), (normed.shape[0], ROWS))
            summed[0] = order(
                summed[0] + jnp.dot(part, block, preferred_element_type=jnp.float32)
            )

    first, second = ring_pairs(True), ring_pairs(False)
    inner = (z == 1) | (z == 2)

    own = order(own_copy.astype(jnp.bfloat16))
    z1 = send("Z1", own, "zero", swap(1))
    m1 = send("M1", own, BOTH, middle_swap())
    a0 = send("A0", own, BOTH, first)
    b0 = send("B0", own, BOTH, second)
    keep, give = split(order(outer_params - own_copy), core == 1)
    k1 = send("K1", order(give), "island", swap(1))
    a0 = order(a0)
    c0 = send("C0", a0, BOTH, second)
    b0 = order(b0)
    m1 = order(m1)
    e2 = send("E2", m1, "zero", swap(1))
    z1 = order(z1)
    m2 = send("M2", z1, BOTH, middle_swap())
    a1 = send("A1", z1, BOTH, first)
    total = order(keep + order(k1))
    keep, give = split(total, x % 2 == 1)
    k2 = send("K2", order(give), "island", swap(2))
    normed = order(normalise(tokens, order(norm_gain[None])))
    total = order(keep + order(k2))
    c0 = order(c0)
    m2 = order(m2)
    s2 = order(jnp.where(inner, m2, order(e2)))
    a2 = send("A2", s2, BOTH, first)
    b2 = send("B2", s2, BOTH, second)
    e3 = send("E3", m2, "zero", swap(1))
    a1 = order(a1)
    keep, give = split(total, x // 2 == 1)
    k3 = send("K3", order(give), "island", swap(4))
    add_product("dot0", own, y, z)
    add_product("dot0", a0, near_y, z)
    total = order(keep + order(k3))
    high = send("HIGH", order(total), "island", swap(8))
    rest = order(jnp.concatenate([b0, c0]))
    a2 = order(a2)
    c2 = send("C2", a2, BOTH, second)
    s3 = order(jnp.where(inner, m1, order(e3)))
    a3 = send("A3", s3, BOTH, first)
    b3 = send("B3", s3, BOTH, second)
    rest = send("ZBC", order(rest), "zero", swap(1))
    add_product("dot0", b0, far_y, z)
    add_product("dot0", c0, y ^ 2, z)
    add_product("dot1", z1, y, z ^ 1)
    add_product("dot1", a1, near_y, z ^ 1)
    add_product("dot2", s2, y, z ^ 2)
    total = order(total + order(high))
    k4 = send("K4", total, "island", swap(4))
    b2 = order(b2)
    add_product("dot2", a2, near_y, z ^ 2)
    add_product("dot2", b2, far_y, z ^ 2)
    add_product("dot3", s3, y, z ^ 3)
    total = order(join(total, order(k4), x // 2 == 1))
    k5 = send("K5", total, "island", swap(2))
    a3 = order(a3)
    c3 = send("C3", a3, BOTH, second)
    add_product("dot3", a3, near_y, z ^ 3)
    add_product("dot2", order(c2), y ^ 2, z ^ 2)
    total = order(join(total, order(k5), x % 2 == 1))
    k6 = send("K6", total, "island", swap(1))
    rest = order(rest)
    add_product("dot1", rest[:ROWS], far_y, z ^ 1)
    add_product("dot1", rest[ROWS:], y ^ 2, z ^ 1)
    add_product("dot3", order(b3), far_y, z ^ 3)
    add_product("dot3", order(c3), y ^ 2, z ^ 3)
    keys = order((summed[0] * (1.0 / math.sqrt(D))).astype(jnp.bfloat16))
    total = order(join(total, order(k6), core == 1))
    islands = lax.axis_size("island")
    params_out, momentum_out = outer_update(outer_params, momentum, total / islands)
    mixed = mix_share * local_weights + (1.0 - mix_share) * params_out[None]
    return (keys, params_out, momentum_out, mixed)


def solution(mesh):
    placed = (
        P(("island", "zero"), None),
        P(),
        P("zero", None),
        P("zero", None),
        P("island", "zero", None),
    )
    return jax.shard_map(
        body,
        mesh=mesh,
        in_specs=placed,
        out_specs=(
            P(("island", "zero"), None),
            P("zero", None),
            P("zero", None),
            P("island", "zero", None),
        ),
        check_vma=False,
    )
```

```python
import math

import jax
import jax.numpy as jnp
from jax import lax
from jax.experimental import pallas as pl
from jax.experimental.pallas import tpu as pltpu
from jax.sharding import PartitionSpec as P

D = 8192
ROWS = 512

epsilon = 1e-05
outer_momentum = 0.9
outer_rate = 0.7
mix_share = 0.5


def ring_pairs(first):
    pairs = []
    for island in range(16):
        for zero in range(16):
            y, z = divmod(zero, 4)
            partner = y ^ 1 if (island % 2 == 0) == first else 3 - y
            pairs.append((island * 16 + zero, island * 16 + partner * 4 + z))
    return pairs


def swap(bits):
    return [(i, i ^ bits) for i in range(16)]


def middle_swap():
    pairs = []
    for island in range(16):
        for zero in range(16):
            y, z = divmod(zero, 4)
            inner = z in (1, 2)
            target = (island, y * 4 + 3 - z) if inner else (island ^ 1, zero)
            pairs.append((island * 16 + zero, target[0] * 16 + target[1]))
    return pairs


BOTH = ("island", "zero")


class Order:
    def __init__(self):
        self.last = None

    def __call__(self, value):
        if self.last is not None:
            value = lax.optimization_barrier((value, self.last))[0]
        self.last = value
        return value


def outer_update(params_part, momentum_part, delta):
    momentum_new = outer_momentum * momentum_part + delta
    params_new = params_part - outer_rate * (delta + outer_momentum * momentum_new)
    return (params_new, momentum_new)


CHUNK = 64
DEPTH = 4


def norm_kernel(tokens_ref, gain_ref, normed_ref, held, arrived):
    step, steps = pl.program_id(0), pl.num_programs(0)

    def fetch(i):
        rows = pl.ds(pl.multiple_of(i * CHUNK, CHUNK), CHUNK)
        slot = lax.rem(i, DEPTH)
        return pltpu.make_async_copy(tokens_ref.at[rows, :], held.at[slot], arrived.at[slot])

    @pl.when(step == 0)
    def _():
        for i in range(DEPTH - 1):
            fetch(i).start()

    @pl.when(step + DEPTH - 1 < steps)
    def _():
        fetch(step + DEPTH - 1).start()

    fetch(step).wait()
    values = held[lax.rem(step, DEPTH)].astype(jnp.float32)
    mean = jnp.sum(values * values, axis=-1, keepdims=True) * (1.0 / D)
    scale = lax.rsqrt(mean + epsilon)
    normed_ref[...] = (values * scale * gain_ref[...]).astype(jnp.bfloat16)


def normalise(tokens, gain):
    count, width = tokens.shape
    return pl.pallas_call(
        norm_kernel,
        out_shape=jax.ShapeDtypeStruct(tokens.shape, tokens.dtype),
        grid=(count // CHUNK,),
        in_specs=[
            pl.BlockSpec(memory_space=pltpu.HBM),
            pl.BlockSpec((1, width), lambda i: (0, 0)),
        ],
        out_specs=pl.BlockSpec((CHUNK, width), lambda i: (i, 0)),
        scratch_shapes=[
            pltpu.VMEM((DEPTH, CHUNK, width), tokens.dtype),
            pltpu.SemaphoreType.DMA((DEPTH,)),
        ],
        compiler_params=pltpu.CompilerParams(vmem_limit_bytes=12 * 1024 * 1024),
        cost_estimate=pl.CostEstimate(
            flops=6 * count * width, bytes_accessed=4 * count * width, transcendentals=0
        ),
        name="normalise",
    )(pltpu.with_memory_space_constraint(tokens, pltpu.HBM), gain)


def send(name, value, axis, pairs):
    with jax.named_scope(name):
        return lax.ppermute(value, axis, pairs)


def split(value, high):
    half = value.shape[0] // 2
    low_part, high_part = value[:half], value[half:]
    return jnp.where(high, high_part, low_part), jnp.where(high, low_part, high_part)


def join(mine, other, high):
    return jnp.concatenate([jnp.where(high, other, mine), jnp.where(high, mine, other)])


def body(tokens, norm_gain, outer_params, momentum, local_weights):
    own_copy = local_weights[0]
    me = lax.axis_index("zero")
    y, z = me // 4, me % 4
    island = lax.axis_index("island")
    core, x = island % 2, island // 2 % 4
    near_y = jnp.where(core == 0, y ^ 1, 3 - y)
    far_y = jnp.where(core == 0, 3 - y, y ^ 1)
    order = Order()
    summed = [0.0]

    def add_product(name, block, row, column):
        start = (row * 4 + column) * ROWS
        with jax.named_scope(name):
            part = lax.dynamic_slice(normed, (0, start), (normed.shape[0], ROWS))
            summed[0] = order(
                summed[0] + jnp.dot(part, block, preferred_element_type=jnp.float32)
            )

    first, second = ring_pairs(True), ring_pairs(False)
    inner = (z == 1) | (z == 2)

    own = order(own_copy.astype(jnp.bfloat16))
    z1 = send("Z1", own, "zero", swap(1))
    m1 = send("M1", own, BOTH, middle_swap())
    a0 = send("A0", own, BOTH, first)
    b0 = send("B0", own, BOTH, second)
    keep, give = split(order(outer_params - own_copy), core == 1)
    k1 = send("K1", order(give), "island", swap(1))
    a0 = order(a0)
    c0 = send("C0", a0, BOTH, second)
    b0 = order(b0)
    m1 = order(m1)
    e2 = send("E2", m1, "zero", swap(1))
    z1 = order(z1)
    m2 = send("M2", z1, BOTH, middle_swap())
    a1 = send("A1", z1, BOTH, first)
    total = order(keep + order(k1))
    keep, give = split(total, x % 2 == 1)
    k2 = send("K2", order(give), "island", swap(2))
    normed = order(normalise(tokens, order(norm_gain[None])))
    total = order(keep + order(k2))
    c0 = order(c0)
    m2 = order(m2)
    s2 = order(jnp.where(inner, m2, order(e2)))
    a2 = send("A2", s2, BOTH, first)
    b2 = send("B2", s2, BOTH, second)
    e3 = send("E3", m2, "zero", swap(1))
    a1 = order(a1)
    keep, give = split(total, x // 2 == 1)
    k3 = send("K3", order(give), "island", swap(4))
    add_product("dot0", own, y, z)
    add_product("dot0", a0, near_y, z)
    total = order(keep + order(k3))
    high = send("HIGH", order(total), "island", swap(8))
    rest = order(jnp.concatenate([b0, c0]))
    a2 = order(a2)
    c2 = send("C2", a2, BOTH, second)
    s3 = order(jnp.where(inner, m1, order(e3)))
    a3 = send("A3", s3, BOTH, first)
    b3 = send("B3", s3, BOTH, second)
    rest = send("ZBC", order(rest), "zero", swap(1))
    add_product("dot0", b0, far_y, z)
    add_product("dot0", c0, y ^ 2, z)
    add_product("dot1", z1, y, z ^ 1)
    add_product("dot1", a1, near_y, z ^ 1)
    add_product("dot2", s2, y, z ^ 2)
    total = order(total + order(high))
    k4 = send("K4", total, "island", swap(4))
    b2 = order(b2)
    add_product("dot2", a2, near_y, z ^ 2)
    add_product("dot2", b2, far_y, z ^ 2)
    add_product("dot3", s3, y, z ^ 3)
    total = order(join(total, order(k4), x // 2 == 1))
    k5 = send("K5", total, "island", swap(2))
    a3 = order(a3)
    c3 = send("C3", a3, BOTH, second)
    add_product("dot3", a3, near_y, z ^ 3)
    add_product("dot2", order(c2), y ^ 2, z ^ 2)
    total = order(join(total, order(k5), x % 2 == 1))
    k6 = send("K6", total, "island", swap(1))
    rest = order(rest)
    add_product("dot1", rest[:ROWS], far_y, z ^ 1)
    add_product("dot1", rest[ROWS:], y ^ 2, z ^ 1)
    add_product("dot3", order(b3), far_y, z ^ 3)
    part = lax.dynamic_slice(
        normed, (0, ((y ^ 2) * 4 + (z ^ 3)) * ROWS), (normed.shape[0], ROWS)
    )
    last = jnp.dot(part, order(c3), preferred_element_type=jnp.float32)
    keys = order(((summed[0] + last) * (1.0 / math.sqrt(D))).astype(jnp.bfloat16))
    total = order(join(total, order(k6), core == 1))
    islands = lax.axis_size("island")
    params_out, momentum_out = outer_update(outer_params, momentum, total / islands)
    mixed = mix_share * local_weights + (1.0 - mix_share) * params_out[None]
    return (keys, params_out, momentum_out, mixed)


def solution(mesh):
    placed = (
        P(("island", "zero"), None),
        P(),
        P("zero", None),
        P("zero", None),
        P("island", "zero", None),
    )
    return jax.shard_map(
        body,
        mesh=mesh,
        in_specs=placed,
        out_specs=(
            P(("island", "zero"), None),
            P("zero", None),
            P("zero", None),
            P("island", "zero", None),
        ),
        check_vma=False,
    )
```
